32 devices in a mesh: dom: 2 (over x), hst: 16 (over z, y, core).
Axes of the slice: x: 2, y: 2, z: 4, core: 2. Of those that a mesh axis runs over, the one named last changes fastest.
Arguments:
- queries: bfloat16 [8192, 4096], P(('dom', 'hst')), parts along dimension 0, may hold values from -96 to 96
- suf_keys: bfloat16 [8192, 512], P(('dom', 'hst')), parts along dimension 0, may hold values from -4 to 4
- suf_values: bfloat16 [8192, 512], P(('dom', 'hst')), parts along dimension 0, may hold values from -30 to 30
- cache_keys: bfloat16 [1024, 16, 512], P(('dom', 'hst')), parts along dimension 0, may hold values from -6 to 6
- cache_values: bfloat16 [1024, 16, 512], P(('dom', 'hst')), parts along dimension 0, may hold values from -30 to 30
- fetch_owner: int32 [32, 128], P(('dom', 'hst')), parts along dimension 0, may hold values from 0 to 15, as said below
- fetch_page: int32 [32, 128], P(('dom', 'hst')), parts along dimension 0, may hold values from 0 to 31
- prefix_len: int32 [32], P(('dom', 'hst')), parts along dimension 0, may hold values from 1 to 2048, as said below
Outputs:
- attended: bfloat16 [8192, 4096], P(('dom', 'hst')), parts along dimension 0
The draws below stay inside these ranges and needn't reach their ends.
There are 2 independent parts, one for each index of `dom`. The reference program is written for one: setup_inputs(seed, part) draws one part's arguments, and reference() takes and returns one part's arrays. A program takes and returns all parts, laid end to end along the dimension named above; each array names one. Nothing has to cross between parts.
Inputs may be any that keep to these rules, and one draw needn't show every extreme that they name: `fetch_owner`: each request's row names every device exactly 8 times. `prefix_len`: in every draw at least one request has a prefix of exactly 2048 tokens, filling all its page slots.
All inputs are finite; a program needn't handle non-finite values.
Results may differ from the reference program's by a relative error of at most 0.0055.
Values may be sent and summed in bfloat16 or wider, within the bound.
A program may use at most 64 MiB of HBM per device.

```python
import jax
import jax.numpy as jnp
from jax import lax

QH = 32
KVH = 4
HD = 128
PAGE = 16
MAXP = 128
SUF = 256
OWN_DEV = 32
READERS = 16
TOKENS = 4096
PAGES = 512


def shared_keys(key):
    return jnp.clip(jax.random.normal(key, (TOKENS, KVH * HD), jnp.float32), -4.0, 4.0)


def draw_suf_keys(key, part):
    key_base = shared_keys(key)
    return key_base.astype(jnp.bfloat16)


def draw_queries(key, part):
    key = jax.random.fold_in(key, 12)
    values = 1.5 * jnp.clip(jax.random.normal(key, (TOKENS, QH * HD), jnp.float32), -6.0, 6.0)
    return values.astype(jnp.bfloat16)


def draw_fetch_owner(key, part):
    key = jax.random.fold_in(key, 21)
    reader_keys = jax.random.split(key, READERS)

    def shuffle(one_key):
        return jax.random.permutation(one_key, MAXP)
    orders = jax.vmap(shuffle)(reader_keys)
    return (orders % READERS).astype(jnp.int32)


def draw_prefix_len(key, part):
    key = jax.random.fold_in(key, 31)
    length_key, pick_key = jax.random.split(key)
    lengths = jax.random.randint(length_key, (READERS,), 1, MAXP * PAGE + 1)
    longest = jax.random.randint(pick_key, (), 0, READERS)
    return jnp.where(jnp.arange(READERS) == longest, MAXP * PAGE, lengths).astype(jnp.int32)


def set_ends(drawn, key, least, largest):
    place = [jax.random.randint(jax.random.fold_in(key, axis), (), 0, length) for axis, length in enumerate(drawn.shape)]
    main_axis = drawn.shape.index(max(drawn.shape))
    neighbour = place[:main_axis] + [(place[main_axis] + 1) % drawn.shape[main_axis]] + place[main_axis + 1:]
    return drawn.at[tuple(place)].set(least).at[tuple(neighbour)].set(largest)


def steps_of(own_key, dims, cuts, low, top_value):
    def one(axis_at, blocks):
        steps = jax.random.uniform(jax.random.fold_in(jax.random.fold_in(own_key, 6), axis_at), (blocks,), jnp.float32, low / len(cuts), top_value / len(cuts))
        return jnp.repeat(jnp.exp(steps), dims[axis_at] // blocks).reshape((-1,) + (1,) * (len(dims) - axis_at - 1))

    gain = one(*cuts[0])
    for cut in cuts[1:]:
        gain = gain * one(*cut)
    return gain


def normal_values(key, dims, scale, most, cuts=(), held_as=jnp.bfloat16):
    gain = steps_of(key, dims, cuts, -0.22, 0.18) if cuts else 1.0
    array = jax.random.normal(key, dims, jnp.float32) * scale * gain
    return jnp.minimum(jnp.maximum(array, -most), most).astype(held_as)


def setup_inputs(seed: int = 0, part: int = 0) -> dict:
    splits = jax.random.split(jax.random.key(seed), 9)
    part_keys = jax.random.split(jax.random.fold_in(splits[8], part), 9)
    queries = draw_queries(jax.random.fold_in(jax.random.fold_in(splits[8], part), 71), part)
    suf_keys = draw_suf_keys(jax.random.fold_in(jax.random.fold_in(splits[8], part), 71), part)
    suf_values = normal_values(part_keys[2], (TOKENS, KVH * HD), 6.0, 30.0, ((0, 16),))
    cache_keys = normal_values(part_keys[3], (PAGES, PAGE, KVH * HD), 1.0, 6.0, ((0, 16),))
    cache_values = normal_values(part_keys[4], (PAGES, PAGE, KVH * HD), 6.0, 30.0, ((0, 16),))
    fetch_owner = draw_fetch_owner(jax.random.fold_in(jax.random.fold_in(splits[8], part), 71), part)
    fetch_page = set_ends(jax.random.randint(part_keys[6], (READERS, MAXP), 0, OWN_DEV), jax.random.fold_in(part_keys[6], 1), 0, OWN_DEV - 1).astype(jnp.int32)
    prefix_len = draw_prefix_len(jax.random.fold_in(jax.random.fold_in(splits[8], part), 71), part)
    return dict(queries=queries, suf_keys=suf_keys, suf_values=suf_values, cache_keys=cache_keys, cache_values=cache_values, fetch_owner=fetch_owner, fetch_page=fetch_page, prefix_len=prefix_len)


MASKED = -1.0e30


def partial_terms(query_rows, key_rows, value_rows, visible, score_scale):
    scores = lax.dot_general(query_rows, key_rows, (((1,), (1,)), ((), ())), preferred_element_type=jnp.float32) * score_scale
    scores = jnp.where(visible, scores, MASKED)
    row_max = jnp.max(scores, axis=1)
    weights = jnp.where(visible, jnp.exp(scores - row_max[:, None]), jnp.float32(0.0))
    weight_sum = jnp.sum(weights, axis=1)
    summed = jnp.dot(weights.astype(jnp.bfloat16), value_rows, preferred_element_type=jnp.float32)
    return row_max, weight_sum, summed


def reference(queries, suf_keys, suf_values, cache_keys, cache_values, fetch_owner, fetch_page, prefix_len):
    group_size = QH // KVH
    score_scale = HD ** -0.5
    key_slot = fetch_owner * OWN_DEV + fetch_page
    prefix_pos = jnp.arange(MAXP * PAGE, dtype=jnp.int32)
    suffix_ids = jnp.arange(SUF, dtype=jnp.int32)
    row_token = jnp.arange(SUF * group_size, dtype=jnp.int32) // group_size

    def one_reader(reader):
        page_table = key_slot[reader]
        length = prefix_len[reader]
        first_row = (reader * SUF).astype(jnp.int32)
        prefix_keys = cache_keys[page_table].reshape(MAXP * PAGE, KVH * HD)
        prefix_values = cache_values[page_table].reshape(MAXP * PAGE, KVH * HD)
        own_queries = lax.dynamic_slice_in_dim(queries, first_row, SUF, 0)
        own_keys = lax.dynamic_slice_in_dim(suf_keys, first_row, SUF, 0)
        own_values = lax.dynamic_slice_in_dim(suf_values, first_row, SUF, 0)
        key_rows = jnp.concatenate([prefix_keys, own_keys], axis=0)
        value_rows = jnp.concatenate([prefix_values, own_values], axis=0)
        prefix_ok = jnp.broadcast_to((prefix_pos < length)[None, :], (SUF * group_size, MAXP * PAGE))
        causal = suffix_ids[None, :] <= row_token[:, None]
        visible = jnp.concatenate([prefix_ok, causal], axis=1)
        results = []
        for kv_head in range(KVH):
            query_rows = own_queries[:, kv_head * group_size * HD:(kv_head + 1) * group_size * HD].reshape(SUF * group_size, HD)
            row_max, weight_sum, summed = partial_terms(query_rows, key_rows[:, kv_head * HD:(kv_head + 1) * HD], value_rows[:, kv_head * HD:(kv_head + 1) * HD], visible, score_scale)
            results.append((summed / weight_sum[:, None]).reshape(SUF, group_size * HD))
        return jnp.concatenate(results, axis=1).astype(jnp.bfloat16)

    attended = lax.map(one_reader, jnp.arange(READERS, dtype=jnp.int32))
    return attended.reshape(TOKENS, QH * HD)
```

```python
import functools

import jax
import jax.numpy as jnp
from jax import lax
from jax.experimental import pallas as pl
from jax.experimental.pallas import tpu as pltpu
from jax.sharding import PartitionSpec as P

HD = 128


MASKED = -1e30


def partial_terms(query_rows, key_rows, value_rows, visible, score_scale):
    scores = (
        lax.dot_general(
            query_rows, key_rows, (((1,), (1,)), ((), ())), preferred_element_type=jnp.float32
        )
        * score_scale
    )
    scores = jnp.where(visible, scores, MASKED)
    row_max = jnp.max(scores, axis=1)
    weights = jnp.where(visible, jnp.exp(scores - row_max[:, None]), jnp.float32(0.0))
    weight_sum = jnp.sum(weights, axis=1)
    summed = jnp.dot(weights.astype(jnp.bfloat16), value_rows, preferred_element_type=jnp.float32)
    return (row_max, weight_sum, summed)


def blocked_terms(query_rows, row_token, key_rows, value_rows, visible_for, score_scale):
    row_count = query_rows.shape[0]
    block_rows = min(512, row_count)
    block_count = row_count // block_rows
    row_blocks = query_rows.reshape(block_count, block_rows, query_rows.shape[1])
    token_blocks = row_token.reshape(block_count, block_rows)

    def one_block(block_pair):
        return partial_terms(
            block_pair[0], key_rows, value_rows, visible_for(block_pair[1]), score_scale
        )

    row_max, weight_sum, summed = lax.map(one_block, (row_blocks, token_blocks))
    return (
        row_max.reshape(row_count),
        weight_sum.reshape(row_count),
        summed.reshape(row_count, -1),
    )


def shards(
    queries, suf_keys, suf_values, cache_keys, cache_values, fetch_owner, fetch_page, prefix_len
):
    host_count = lax.axis_size("hst")
    own_index = lax.axis_index("hst")
    slot_count = fetch_owner.shape[1]
    capacity = slot_count // host_count
    page_rows = cache_keys.shape[1]
    kv_width = cache_keys.shape[2]
    suffix = queries.shape[0]
    kv_heads = kv_width // HD
    group_size = queries.shape[1] // kv_width
    score_scale = HD ** (-0.5)
    owners = fetch_owner[0]
    length = prefix_len[0]
    peer_ids = jnp.arange(host_count, dtype=jnp.int32)
    owner_hits = (owners[:, None] == peer_ids[None, :]).astype(jnp.int32)
    before = jnp.cumsum(owner_hits, axis=0) - owner_hits
    owner_rank = jnp.sum(before * owner_hits, axis=1)
    slot_of = owners * capacity + owner_rank
    slot_ids = jnp.arange(slot_count, dtype=jnp.int32)
    slot_match = (slot_of[None, :] == slot_ids[:, None]).astype(jnp.int32)
    position = jnp.sum(slot_match * slot_ids[None, :], axis=1)
    all_owners, all_pages = (
        lax.all_gather(fetch_owner, "hst", axis=0, tiled=True),
        lax.all_gather(fetch_page, "hst", axis=0, tiled=True),
    )
    from_me = (all_owners == own_index).astype(jnp.int32)
    send_rank = jnp.cumsum(from_me, axis=1) - from_me
    level_ids = jnp.arange(capacity, dtype=jnp.int32)
    picked = from_me[:, :, None] * (send_rank[:, :, None] == level_ids[None, None, :]).astype(
        jnp.int32
    )
    served = jnp.sum(picked * all_pages[:, :, None], axis=1)
    flat_served = served.reshape(-1)
    sent_keys = cache_keys[flat_served].reshape(host_count, capacity, page_rows, kv_width)
    sent_values = cache_values[flat_served].reshape(host_count, capacity, page_rows, kv_width)
    row_token = jnp.arange(suffix * group_size, dtype=jnp.int32) // group_size
    suffix_ids = jnp.arange(suffix, dtype=jnp.int32)
    page_offsets = jnp.arange(page_rows, dtype=jnp.int32)
    head_rows = [
        queries[:, kv_head * group_size * HD : (kv_head + 1) * group_size * HD].reshape(
            suffix * group_size, HD
        )
        for kv_head in range(kv_heads)
    ]

    def causal_for(block_tokens):
        return suffix_ids[None, :] <= block_tokens[:, None]

    got_keys, got_values = (
        lax.all_to_all(
            sent_keys.reshape(host_count, capacity * page_rows, kv_width),
            "hst",
            split_axis=0,
            concat_axis=0,
            tiled=True,
        ),
        lax.all_to_all(
            sent_values.reshape(host_count, capacity * page_rows, kv_width),
            "hst",
            split_axis=0,
            concat_axis=0,
            tiled=True,
        ),
    )
    key_rows = jnp.concatenate(
        [got_keys.reshape(slot_count * page_rows, kv_width), suf_keys], axis=0
    )
    value_rows = jnp.concatenate(
        [got_values.reshape(slot_count * page_rows, kv_width), suf_values], axis=0
    )
    prefix_ok = (position[:, None] * page_rows + page_offsets[None, :]).reshape(-1) < length

    def visible_for(block_tokens):
        prefix_part = jnp.broadcast_to(
            prefix_ok[None, :], (block_tokens.shape[0], prefix_ok.shape[0])
        )
        return jnp.concatenate([prefix_part, causal_for(block_tokens)], axis=1)

    states = [
        blocked_terms(
            head_rows[kv_head],
            row_token,
            key_rows[:, kv_head * HD : (kv_head + 1) * HD],
            value_rows[:, kv_head * HD : (kv_head + 1) * HD],
            visible_for,
            score_scale,
        )
        for kv_head in range(kv_heads)
    ]
    results = [(state[2] / state[1][:, None]).reshape(suffix, group_size * HD) for state in states]
    return jnp.concatenate(results, axis=1).astype(jnp.bfloat16)


PLANE = 4
LOG2E = 1.4426950408889634
VMEM_BYTES = 56 * 2**20
MESH = pl.DeviceIdType.MESH


def arrival(source, here, line):
    far = jnp.abs(source - here)
    nearer = jnp.minimum(far - 1, here) + jnp.minimum(far - 1, line - 1 - here)
    after_twin = jnp.logical_and(source > here, here - far >= 0).astype(jnp.int32)
    return nearer + after_twin + 1


def source_of(turn, here, line):
    found = jnp.int32(0)
    for candidate in range(line):
        match = jnp.logical_and(candidate != here, arrival(jnp.int32(candidate), here, line) == turn)
        found = found + jnp.where(match, candidate, 0)
    return found


def fused_kernel(
    line,
    capacity,
    page_rows,
    q_ref,
    sk_ref,
    sv_ref,
    ck_ref,
    cv_ref,
    table_ref,
    bias_ref,
    o_ref,
    tables,
    pages_smem,
    line_buf,
    picked_from,
    stage,
    got,
    m_ref,
    acc_ref,
    table_send,
    table_recv,
    local_sem,
    own_send,
    line_send,
    line_recv,
    plane_send,
    plane_recv,
):
    me = lax.axis_index("hst")
    here = me // PLANE
    place = lax.rem(me, PLANE)
    suffix = q_ref.shape[0]
    heads = q_ref.shape[1] // HD
    kv_width = sk_ref.shape[1]
    group_heads = heads // (kv_width // HD)
    chunk = capacity * page_rows
    factor = HD ** (-0.5) * LOG2E
    caches = (ck_ref, cv_ref)

    def partner(step):
        return lax.rem(place + step, PLANE)

    def plane_id(where):
        return {"hst": here * PLANE + where}

    def line_id(where):
        return {"hst": where * PLANE + place}

    has_side = (here > 0, here < line - 1)
    toward = (here - 1, here + 1)

    barrier = pltpu.get_barrier_semaphore()
    for step in range(1, PLANE):
        pl.semaphore_signal(barrier, inc=1, device_id=plane_id(partner(step)), device_id_type=MESH)
    for side in range(2):

        @pl.when(has_side[side])
        def _():
            pl.semaphore_signal(barrier, inc=1, device_id=line_id(toward[side]), device_id_type=MESH)

    sides = has_side[0].astype(jnp.int32) + has_side[1].astype(jnp.int32)
    pl.semaphore_wait(barrier, PLANE - 1 + sides)

    def own_copy(side, kind):
        return pltpu.make_async_remote_copy(
            src_ref=caches[kind],
            dst_ref=line_buf.at[1 - side, 0, kind],
            send_sem=own_send.at[side, kind],
            recv_sem=line_recv.at[1 - side, 0, kind],
            device_id=line_id(toward[side]),
            device_id_type=MESH,
        )

    def forward_copy(side, far, kind):
        return pltpu.make_async_remote_copy(
            src_ref=line_buf.at[side, far - 1, kind],
            dst_ref=line_buf.at[side, far, kind],
            send_sem=line_send.at[side, far - 1, kind],
            recv_sem=line_recv.at[side, far, kind],
            device_id=line_id(toward[1 - side]),
            device_id_type=MESH,
        )

    def table_copy(step):
        return pltpu.make_async_remote_copy(
            src_ref=table_ref,
            dst_ref=tables.at[place],
            send_sem=table_send.at[step - 1],
            recv_sem=table_recv.at[place],
            device_id=plane_id(partner(step)),
            device_id_type=MESH,
        )

    def plane_copy(turn, kind, step):
        return pltpu.make_async_remote_copy(
            src_ref=stage.at[turn, kind, step - 1],
            dst_ref=got.at[turn, kind, place],
            send_sem=plane_send.at[turn, kind, step - 1],
            recv_sem=plane_recv.at[turn, kind, place],
            device_id=plane_id(partner(step)),
            device_id_type=MESH,
        )

    for step in range(1, PLANE):
        table_copy(step).start()
    for kind in range(2):
        for side in range(2):

            @pl.when(has_side[side])
            def _():
                own_copy(side, kind).start()

    own_table = pltpu.make_async_copy(table_ref, tables.at[place], local_sem.at[0])
    own_table.start()
    own_table.wait()
    for step in range(1, PLANE):
        from_there = pltpu.make_async_remote_copy(
            src_ref=table_ref,
            dst_ref=tables.at[partner(step)],
            send_sem=table_send.at[step - 1],
            recv_sem=table_recv.at[partner(step)],
            device_id=plane_id(partner(step)),
            device_id_type=MESH,
        )
        from_there.wait()
    to_smem = pltpu.make_async_copy(tables, pages_smem, local_sem.at[1])
    to_smem.start()
    to_smem.wait()

    def pick_and_send(source, turn, kind, from_ref):
        first = (source * PLANE + place) * capacity
        for step in range(1, PLANE):
            who = partner(step)

            def one_page(j, carry):
                page = pages_smem[who, 0, first + j]
                stage[turn, kind, step - 1, pl.ds(pl.multiple_of(j * page_rows, page_rows), page_rows)] = (
                    from_ref[page]
                )
                return carry

            lax.fori_loop(0, capacity, one_page, 0, unroll=True)
            plane_copy(turn, kind, step).start()

        def own_page(j, carry):
            page = pages_smem[place, 0, first + j]
            got[turn, kind, place, pl.ds(pl.multiple_of(j * page_rows, page_rows), page_rows)] = from_ref[
                page
            ]
            return carry

        lax.fori_loop(0, capacity, own_page, 0, unroll=True)

    def event(far, kind):
        for side in range(2):
            source = here - far if side == 0 else here + far
            valid = source >= 0 if side == 0 else source < line

            @pl.when(valid)
            def _():
                pltpu.make_async_remote_copy(
                    src_ref=line_buf.at[side, far - 1, kind],
                    dst_ref=line_buf.at[side, far - 1, kind],
                    send_sem=line_send.at[side, far - 1, kind],
                    recv_sem=line_recv.at[side, far - 1, kind],
                    device_id=line_id(source),
                    device_id_type=MESH,
                ).wait_recv()
                if far < line - 1:

                    @pl.when(has_side[1 - side])
                    def _():
                        forward_copy(side, far, kind).start()

                picked_from[...] = line_buf[side, far - 1, kind]
                pick_and_send(source, arrival(source, here, line), kind, picked_from)

    def wait_plane(turn, kind):
        for step in range(1, PLANE):
            there = partner(step)
            pltpu.make_async_remote_copy(
                src_ref=stage.at[turn, kind, step - 1],
                dst_ref=got.at[turn, kind, there],
                send_sem=plane_send.at[turn, kind, step - 1],
                recv_sem=plane_recv.at[turn, kind, there],
                device_id=plane_id(there),
                device_id_type=MESH,
            ).wait()

    def attend(first_head, last_head, key_of, value_of, bias_of, count, first, last):
        width = 2

        def heads_step(pair, carry):
            base = first_head + pair * width
            kv_head = base // group_heads
            columns = pl.ds(pl.multiple_of(kv_head * HD, HD), HD)
            key_rows = key_of(columns)
            value_rows = value_of(columns)
            values = jnp.concatenate([value_rows, jnp.ones_like(value_rows)], axis=1)
            for inner in range(width):
                head = base + inner
                head_columns = pl.ds(pl.multiple_of(head * HD, HD), HD)
                scores = lax.dot_general(
                    q_ref[:, head_columns],
                    key_rows,
                    (((1,), (1,)), ((), ())),
                    preferred_element_type=jnp.float32,
                )
                scores = bias_of(scores * factor)
                top = jnp.max(scores, axis=1, keepdims=True)
                if first:
                    new_max = jnp.broadcast_to(top, (suffix, HD))
                else:
                    old_max = m_ref[head]
                    new_max = jnp.maximum(old_max, top)
                weights = jnp.concatenate(
                    [
                        jnp.exp2(scores[:, tile * HD : (tile + 1) * HD] - new_max).astype(jnp.bfloat16)
                        for tile in range(count // HD)
                    ],
                    axis=1,
                )
                summed = jnp.dot(weights, values, preferred_element_type=jnp.float32)
                if not first:
                    shrink = jnp.exp2(old_max - new_max)
                    summed = acc_ref[head] * jnp.concatenate([shrink, shrink], axis=1) + summed
                if last:
                    o_ref[:, head_columns] = (summed[:, :HD] / summed[:, HD:]).astype(jnp.bfloat16)
                else:
                    acc_ref[head] = summed
                    m_ref[head] = new_max
            return carry

        lax.fori_loop(0, (last_head - first_head) // width, heads_step, 0)

    def attend_suffix():
        causal = lax.broadcasted_iota(jnp.int32, (suffix, suffix), 1) <= lax.broadcasted_iota(
            jnp.int32, (suffix, suffix), 0
        )
        attend(
            0,
            heads,
            lambda columns: sk_ref[:, columns],
            lambda columns: sv_ref[:, columns],
            lambda scores: jnp.where(causal, scores, MASKED),
            suffix,
            True,
            False,
        )

    def attend_group(turn, source, first_head, last_head, last):
        bias = bias_ref[source]

        def rows_of(kind):
            return lambda columns: got[turn, kind, :, :, columns].reshape(PLANE * chunk, HD)

        attend(
            first_head,
            last_head,
            rows_of(0),
            rows_of(1),
            lambda scores: scores + bias,
            PLANE * chunk,
            False,
            last,
        )

    pick_and_send(here, 0, 0, ck_ref)
    pick_and_send(here, 0, 1, cv_ref)
    attend_suffix()
    wait_plane(0, 0)
    wait_plane(0, 1)
    for turn in range(1, line):
        before = here if turn == 1 else source_of(turn - 1, here, line)
        event(turn, 0)
        attend_group(turn - 1, before, 0, heads // 2, False)
        event(turn, 1)
        attend_group(turn - 1, before, heads // 2, heads, False)
        wait_plane(turn, 0)
        wait_plane(turn, 1)
    attend_group(line - 1, source_of(line - 1, here, line), 0, heads, True)

    for kind in range(2):
        for side in range(2):

            @pl.when(has_side[side])
            def _():
                own_copy(side, kind).wait_send()

            for far in range(1, line - 1):
                source = here - far if side == 0 else here + far
                valid = source >= 0 if side == 0 else source < line

                @pl.when(jnp.logical_and(valid, has_side[1 - side]))
                def _():
                    forward_copy(side, far, kind).wait_send()


def fused(queries, suf_keys, suf_values, cache_keys, cache_values, fetch_owner, fetch_page, prefix_len):
    host_count = lax.axis_size("hst")
    line = host_count // PLANE
    slot_count = fetch_owner.shape[1]
    capacity = slot_count // host_count
    own_pages, page_rows, kv_width = cache_keys.shape
    suffix = queries.shape[0]
    heads = queries.shape[1] // HD
    owners = fetch_owner[0]
    slot_ids = jnp.arange(slot_count, dtype=jnp.int32)
    earlier = jnp.logical_and(
        owners[None, :] == owners[:, None], slot_ids[None, :] < slot_ids[:, None]
    )
    rank = jnp.sum(earlier.astype(jnp.int32), axis=1)
    slot_of = owners * capacity + rank
    match = slot_of[None, :] == slot_ids[:, None]
    pages = jnp.sum(jnp.where(match, fetch_page, 0), axis=1)
    position = jnp.sum(jnp.where(match, slot_ids[None, :], 0), axis=1)
    table = jnp.broadcast_to(pages[None, :], (8, slot_count))
    row_ids = jnp.arange(page_rows, dtype=jnp.int32)
    seen = position[:, None] * page_rows + row_ids[None, :] < prefix_len[0]
    bias = jnp.where(seen, jnp.float32(0.0), jnp.float32(MASKED)).reshape(line, 1, PLANE * capacity * page_rows)
    vmem = pl.BlockSpec(memory_space=pltpu.VMEM)
    chunk = capacity * page_rows
    shard = (own_pages, page_rows, kv_width)
    dma = pltpu.SemaphoreType.DMA
    return pl.pallas_call(
        functools.partial(fused_kernel, line, capacity, page_rows),
        out_shape=jax.ShapeDtypeStruct(queries.shape, jnp.bfloat16),
        in_specs=[vmem] * 7,
        out_specs=vmem,
        scratch_shapes=[
            pltpu.VMEM((PLANE, 8, slot_count), jnp.int32),
            pltpu.SMEM((PLANE, 8, slot_count), jnp.int32),
            pltpu.VMEM((2, line - 1, 2) + shard, jnp.bfloat16),
            pltpu.VMEM(shard, jnp.bfloat16),
            pltpu.VMEM((line, 2, PLANE - 1, chunk, kv_width), jnp.bfloat16),
            pltpu.VMEM((line, 2, PLANE, chunk, kv_width), jnp.bfloat16),
            pltpu.VMEM((heads, suffix, HD), jnp.float32),
            pltpu.VMEM((heads, suffix, 2 * HD), jnp.float32),
            dma((PLANE - 1,)),
            dma((PLANE,)),
            dma((2,)),
            dma((2, 2)),
            dma((2, line - 1, 2)),
            dma((2, line - 1, 2)),
            dma((line, 2, PLANE - 1)),
            dma((line, 2, PLANE)),
        ],
        compiler_params=pltpu.CompilerParams(
            collective_id=0, has_side_effects=True, vmem_limit_bytes=VMEM_BYTES
        ),
    )(queries, suf_keys, suf_values, cache_keys, cache_values, table, bias)


def fits(mesh, cache_shape):
    hosts = mesh.shape["hst"]
    own_bytes = 2 * 2 * cache_shape[1] * cache_shape[2] * cache_shape[0] // mesh.size
    return hosts % PLANE == 0 and hosts > PLANE and 2 * (hosts // PLANE - 1) * own_bytes <= 8 * 2**20


def solution(mesh):
    in_specs = (
        P(("dom", "hst"), None),
        P(("dom", "hst"), None),
        P(("dom", "hst"), None),
        P(("dom", "hst"), None, None),
        P(("dom", "hst"), None, None),
        P(("dom", "hst"), None),
        P(("dom", "hst"), None),
        P(("dom", "hst")),
    )
    out_specs = P(("dom", "hst"), None)

    def run(*args):
        body = fused if fits(mesh, args[3].shape) else shards
        return jax.shard_map(
            body, mesh=mesh, in_specs=in_specs, out_specs=out_specs, check_vma=False
        )(*args)

    return run
```

```python
import functools

import jax
import jax.numpy as jnp
from jax import lax
from jax.experimental import pallas as pl
from jax.experimental.pallas import tpu as pltpu
from jax.sharding import PartitionSpec as P

HD = 128


MASKED = -1e30


def partial_terms(query_rows, key_rows, value_rows, visible, score_scale):
    scores = (
        lax.dot_general(
            query_rows, key_rows, (((1,), (1,)), ((), ())), preferred_element_type=jnp.float32
        )
        * score_scale
    )
    scores = jnp.where(visible, scores, MASKED)
    row_max = jnp.max(scores, axis=1)
    weights = jnp.where(visible, jnp.exp(scores - row_max[:, None]), jnp.float32(0.0))
    weight_sum = jnp.sum(weights, axis=1)
    summed = jnp.dot(weights.astype(jnp.bfloat16), value_rows, preferred_element_type=jnp.float32)
    return (row_max, weight_sum, summed)


def blocked_terms(query_rows, row_token, key_rows, value_rows, visible_for, score_scale):
    row_count = query_rows.shape[0]
    block_rows = min(512, row_count)
    block_count = row_count // block_rows
    row_blocks = query_rows.reshape(block_count, block_rows, query_rows.shape[1])
    token_blocks = row_token.reshape(block_count, block_rows)

    def one_block(block_pair):
        return partial_terms(
            block_pair[0], key_rows, value_rows, visible_for(block_pair[1]), score_scale
        )

    row_max, weight_sum, summed = lax.map(one_block, (row_blocks, token_blocks))
    return (
        row_max.reshape(row_count),
        weight_sum.reshape(row_count),
        summed.reshape(row_count, -1),
    )


def shards(
    queries, suf_keys, suf_values, cache_keys, cache_values, fetch_owner, fetch_page, prefix_len
):
    host_count = lax.axis_size("hst")
    own_index = lax.axis_index("hst")
    slot_count = fetch_owner.shape[1]
    capacity = slot_count // host_count
    page_rows = cache_keys.shape[1]
    kv_width = cache_keys.shape[2]
    suffix = queries.shape[0]
    kv_heads = kv_width // HD
    group_size = queries.shape[1] // kv_width
    score_scale = HD ** (-0.5)
    owners = fetch_owner[0]
    length = prefix_len[0]
    peer_ids = jnp.arange(host_count, dtype=jnp.int32)
    owner_hits = (owners[:, None] == peer_ids[None, :]).astype(jnp.int32)
    before = jnp.cumsum(owner_hits, axis=0) - owner_hits
    owner_rank = jnp.sum(before * owner_hits, axis=1)
    slot_of = owners * capacity + owner_rank
    slot_ids = jnp.arange(slot_count, dtype=jnp.int32)
    slot_match = (slot_of[None, :] == slot_ids[:, None]).astype(jnp.int32)
    position = jnp.sum(slot_match * slot_ids[None, :], axis=1)
    all_owners, all_pages = (
        lax.all_gather(fetch_owner, "hst", axis=0, tiled=True),
        lax.all_gather(fetch_page, "hst", axis=0, tiled=True),
    )
    from_me = (all_owners == own_index).astype(jnp.int32)
    send_rank = jnp.cumsum(from_me, axis=1) - from_me
    level_ids = jnp.arange(capacity, dtype=jnp.int32)
    picked = from_me[:, :, None] * (send_rank[:, :, None] == level_ids[None, None, :]).astype(
        jnp.int32
    )
    served = jnp.sum(picked * all_pages[:, :, None], axis=1)
    flat_served = served.reshape(-1)
    sent_keys = cache_keys[flat_served].reshape(host_count, capacity, page_rows, kv_width)
    sent_values = cache_values[flat_served].reshape(host_count, capacity, page_rows, kv_width)
    row_token = jnp.arange(suffix * group_size, dtype=jnp.int32) // group_size
    suffix_ids = jnp.arange(suffix, dtype=jnp.int32)
    page_offsets = jnp.arange(page_rows, dtype=jnp.int32)
    head_rows = [
        queries[:, kv_head * group_size * HD : (kv_head + 1) * group_size * HD].reshape(
            suffix * group_size, HD
        )
        for kv_head in range(kv_heads)
    ]

    def causal_for(block_tokens):
        return suffix_ids[None, :] <= block_tokens[:, None]

    got_keys, got_values = (
        lax.all_to_all(
            sent_keys.reshape(host_count, capacity * page_rows, kv_width),
            "hst",
            split_axis=0,
            concat_axis=0,
            tiled=True,
        ),
        lax.all_to_all(
            sent_values.reshape(host_count, capacity * page_rows, kv_width),
            "hst",
            split_axis=0,
            concat_axis=0,
            tiled=True,
        ),
    )
    key_rows = jnp.concatenate(
        [got_keys.reshape(slot_count * page_rows, kv_width), suf_keys], axis=0
    )
    value_rows = jnp.concatenate(
        [got_values.reshape(slot_count * page_rows, kv_width), suf_values], axis=0
    )
    prefix_ok = (position[:, None] * page_rows + page_offsets[None, :]).reshape(-1) < length

    def visible_for(block_tokens):
        prefix_part = jnp.broadcast_to(
            prefix_ok[None, :], (block_tokens.shape[0], prefix_ok.shape[0])
        )
        return jnp.concatenate([prefix_part, causal_for(block_tokens)], axis=1)

    states = [
        blocked_terms(
            head_rows[kv_head],
            row_token,
            key_rows[:, kv_head * HD : (kv_head + 1) * HD],
            value_rows[:, kv_head * HD : (kv_head + 1) * HD],
            visible_for,
            score_scale,
        )
        for kv_head in range(kv_heads)
    ]
    results = [(state[2] / state[1][:, None]).reshape(suffix, group_size * HD) for state in states]
    return jnp.concatenate(results, axis=1).astype(jnp.bfloat16)


PLANE = 4
WIDTH = 8
TURN_KEYS = False
LOG2E = 1.4426950408889634
VMEM_BYTES = 56 * 2**20
MESH = pl.DeviceIdType.MESH


def arrival(source, here, line):
    far = jnp.abs(source - here)
    nearer = jnp.minimum(far - 1, here) + jnp.minimum(far - 1, line - 1 - here)
    after_twin = jnp.logical_and(source > here, here - far >= 0).astype(jnp.int32)
    return nearer + after_twin + 1


def source_of(turn, here, line):
    found = jnp.int32(0)
    for candidate in range(line):
        match = jnp.logical_and(candidate != here, arrival(jnp.int32(candidate), here, line) == turn)
        found = found + jnp.where(match, candidate, 0)
    return found


def fused_kernel(
    line,
    capacity,
    page_rows,
    q_ref,
    sk_ref,
    sv_ref,
    ck_ref,
    cv_ref,
    owner_ref,
    page_ref,
    len_ref,
    o_ref,
    table_ref,
    tables,
    pages_smem,
    keep_ref,
    line_buf,
    picked_from,
    stage,
    got,
    scaled_q,
    key_block,
    value_block,
    weights_ref,
    m_ref,
    acc_ref,
    table_send,
    table_recv,
    local_sem,
    own_send,
    line_send,
    line_recv,
    plane_send,
    plane_recv,
):
    me = lax.axis_index("hst")
    here = me // PLANE
    place = lax.rem(me, PLANE)
    suffix = q_ref.shape[0]
    heads = q_ref.shape[1] // HD
    kv_width = sk_ref.shape[1]
    group_heads = heads // (kv_width // HD)
    chunk = capacity * page_rows
    factor = HD ** (-0.5) * LOG2E
    caches = (ck_ref, cv_ref)

    def partner(step):
        return lax.rem(place + step, PLANE)

    def plane_id(where):
        return {"hst": here * PLANE + where}

    def line_id(where):
        return {"hst": where * PLANE + place}

    has_side = (here > 0, here < line - 1)
    toward = (here - 1, here + 1)

    barrier = pltpu.get_barrier_semaphore()
    for step in range(1, PLANE):
        pl.semaphore_signal(barrier, inc=1, device_id=plane_id(partner(step)), device_id_type=MESH)
    for side in range(2):

        @pl.when(has_side[side])
        def _():
            pl.semaphore_signal(barrier, inc=1, device_id=line_id(toward[side]), device_id_type=MESH)

    sides = has_side[0].astype(jnp.int32) + has_side[1].astype(jnp.int32)
    pl.semaphore_wait(barrier, PLANE - 1 + sides)

    def make_table():
        slots = owner_ref.shape[1]
        square = (slots, slots)
        down = lax.broadcasted_iota(jnp.int32, square, 0)
        across = lax.broadcasted_iota(jnp.int32, square, 1)
        owner_row = jnp.broadcast_to(owner_ref[...], square)
        owner_column = jnp.transpose(owner_row)
        page_column = jnp.transpose(jnp.broadcast_to(page_ref[...], square))
        same = owner_row == owner_column
        rank_row = jnp.sum(
            jnp.where(jnp.logical_and(same, down < across), 1, 0), axis=0, keepdims=True
        )
        slot_row = jnp.broadcast_to(owner_row[:1] * capacity + rank_row, square)
        slot_column = jnp.transpose(slot_row)
        pages = jnp.sum(
            jnp.where(slot_column == across, page_column, 0), axis=0, keepdims=True
        )
        pages = jnp.clip(pages, 0, ck_ref.shape[0] - 1)
        table_ref[...] = jnp.broadcast_to(pages, table_ref.shape)
        position = jnp.sum(
            jnp.where(slot_row == down, across, 0).astype(jnp.float32),
            axis=1,
            keepdims=True,
        )
        by_row = jnp.broadcast_to(position.reshape(slots, 1, 1), (slots, page_rows, HD))
        in_page = lax.broadcasted_iota(jnp.int32, by_row.shape, 1).astype(jnp.float32)
        limit = len_ref[0].astype(jnp.float32)
        keep = jnp.where(by_row * page_rows + in_page < limit, 1.0, 0.0).astype(jnp.bfloat16)
        keep_ref[...] = keep.reshape(keep_ref.shape)

    def own_copy(side, kind):
        return pltpu.make_async_remote_copy(
            src_ref=caches[kind],
            dst_ref=line_buf.at[1 - side, 0, kind],
            send_sem=own_send.at[side, kind],
            recv_sem=line_recv.at[1 - side, 0, kind],
            device_id=line_id(toward[side]),
            device_id_type=MESH,
        )

    def forward_copy(side, far, kind):
        return pltpu.make_async_remote_copy(
            src_ref=line_buf.at[side, far - 1, kind],
            dst_ref=line_buf.at[side, far, kind],
            send_sem=line_send.at[side, far - 1, kind],
            recv_sem=line_recv.at[side, far, kind],
            device_id=line_id(toward[1 - side]),
            device_id_type=MESH,
        )

    def table_copy(step):
        return pltpu.make_async_remote_copy(
            src_ref=table_ref,
            dst_ref=tables.at[place],
            send_sem=table_send.at[step - 1],
            recv_sem=table_recv.at[place],
            device_id=plane_id(partner(step)),
            device_id_type=MESH,
        )

    def plane_copy(turn, kind, step):
        return pltpu.make_async_remote_copy(
            src_ref=stage.at[turn, kind, step - 1],
            dst_ref=got.at[turn, kind, place],
            send_sem=plane_send.at[turn, kind, step - 1],
            recv_sem=plane_recv.at[turn, kind, place],
            device_id=plane_id(partner(step)),
            device_id_type=MESH,
        )

    for kind in range(2):
        for side in range(2):

            @pl.when(has_side[side])
            def _():
                own_copy(side, kind).start()

    make_table()
    for step in range(1, PLANE):
        table_copy(step).start()

    own_table = pltpu.make_async_copy(table_ref, tables.at[place], local_sem.at[0])
    own_table.start()
    own_table.wait()
    for step in range(1, PLANE):
        from_there = pltpu.make_async_remote_copy(
            src_ref=table_ref,
            dst_ref=tables.at[partner(step)],
            send_sem=table_send.at[step - 1],
            recv_sem=table_recv.at[partner(step)],
            device_id=plane_id(partner(step)),
            device_id_type=MESH,
        )
        from_there.wait()
    to_smem = pltpu.make_async_copy(tables, pages_smem, local_sem.at[1])
    to_smem.start()
    to_smem.wait()

    def pick_and_send(source, turn, kind, from_ref):
        first = (source * PLANE + place) * capacity
        for step in range(1, PLANE):
            who = partner(step)

            def one_page(j, carry):
                page = pages_smem[who, 0, first + j]
                stage[turn, kind, step - 1, pl.ds(pl.multiple_of(j * page_rows, page_rows), page_rows)] = (
                    from_ref[page]
                )
                return carry

            lax.fori_loop(0, capacity, one_page, 0, unroll=True)
            plane_copy(turn, kind, step).start()

        def own_page(j, carry):
            page = pages_smem[place, 0, first + j]
            got[turn, kind, place, pl.ds(pl.multiple_of(j * page_rows, page_rows), page_rows)] = from_ref[
                page
            ]
            return carry

        lax.fori_loop(0, capacity, own_page, 0, unroll=True)

    def event(far, kind):
        for side in range(2):
            source = here - far if side == 0 else here + far
            valid = source >= 0 if side == 0 else source < line

            @pl.when(valid)
            def _():
                pltpu.make_async_remote_copy(
                    src_ref=line_buf.at[side, far - 1, kind],
                    dst_ref=line_buf.at[side, far - 1, kind],
                    send_sem=line_send.at[side, far - 1, kind],
                    recv_sem=line_recv.at[side, far - 1, kind],
                    device_id=line_id(source),
                    device_id_type=MESH,
                ).wait_recv()
                if far < line - 1:

                    @pl.when(has_side[1 - side])
                    def _():
                        forward_copy(side, far, kind).start()

                picked_from[...] = line_buf[side, far - 1, kind]
                pick_and_send(source, arrival(source, here, line), kind, picked_from)

    def wait_plane(turn, kind):
        for step in range(1, PLANE):
            there = partner(step)
            pltpu.make_async_remote_copy(
                src_ref=stage.at[turn, kind, step - 1],
                dst_ref=got.at[turn, kind, there],
                send_sem=plane_send.at[turn, kind, step - 1],
                recv_sem=plane_recv.at[turn, kind, there],
                device_id=plane_id(there),
                device_id_type=MESH,
            ).wait()

    kv_heads = kv_width // HD
    count = PLANE * chunk

    def load_keys(kv_head, key_rows, keep):
        if keep is not None:
            columns = pl.ds(pl.multiple_of(kv_head * HD, HD), HD)
            key_rows = key_rows * keep + sk_ref[0:1, columns] * (1 - keep)
        if TURN_KEYS:
            turned = jnp.transpose(key_rows)
            key_block[0:HD, : key_rows.shape[0]] = turned
            key_block[HD : 2 * HD, : key_rows.shape[0]] = turned
        else:
            key_block[: key_rows.shape[0], :HD] = key_rows
            key_block[: key_rows.shape[0], HD:] = key_rows

    def load_values(value_rows, keep):
        rows = value_rows.shape[0]
        value_block[:rows, :HD] = value_rows if keep is None else value_rows * keep
        value_block[:rows, HD:] = jnp.ones_like(value_rows) if keep is None else keep

    def scores_of(query_rows, keys):
        if TURN_KEYS:
            return jnp.dot(query_rows, key_block[:, :keys], preferred_element_type=jnp.float32)
        return lax.dot_general(
            query_rows, key_block[:keys], (((1,), (1,)), ((), ())), preferred_element_type=jnp.float32
        )

    def each_kv_head(load, one_head):
        def kv_step(kv_head, carry):
            load(kv_head)

            def heads_step(part, inner_carry):
                for inner in range(WIDTH):
                    one_head(kv_head * group_heads + part * WIDTH + inner)
                return inner_carry

            lax.fori_loop(0, group_heads // WIDTH, heads_step, 0)
            return carry

        lax.fori_loop(0, kv_heads, kv_step, 0)

    def weigh(scores, top):
        return jnp.concatenate(
            [
                jnp.exp2(scores[:, tile * HD : (tile + 1) * HD] - top).astype(jnp.bfloat16)
                for tile in range(scores.shape[1] // HD)
            ],
            axis=1,
        )

    def attend_suffix():
        causal = lax.broadcasted_iota(jnp.int32, (suffix, suffix), 1) <= lax.broadcasted_iota(
            jnp.int32, (suffix, suffix), 0
        )

        def load(kv_head):
            columns = pl.ds(pl.multiple_of(kv_head * HD, HD), HD)
            load_keys(kv_head, sk_ref[:, columns], None)
            load_values(sv_ref[:, columns], None)

        def one_head(head):
            scaled = q_ref[:, pl.ds(pl.multiple_of(head * HD, HD), HD)].astype(jnp.float32) * factor
            high = scaled.astype(jnp.bfloat16)
            low = (scaled - high.astype(jnp.float32)).astype(jnp.bfloat16)
            both = jnp.concatenate([high, low], axis=1)
            scaled_q[head] = both
            scores = jnp.where(causal, scores_of(both, suffix), MASKED)
            top = jnp.broadcast_to(jnp.max(scores, axis=1, keepdims=True), (suffix, HD))
            weights = weigh(scores, top)
            m_ref[head] = top
            acc_ref[head] = jnp.dot(weights, value_block[:suffix], preferred_element_type=jnp.float32)

        each_kv_head(load, one_head)

    def group_rows(turn, kind, kv_head):
        columns = pl.ds(pl.multiple_of(kv_head * HD, HD), HD)
        return got[turn, kind, :, :, columns].reshape(count, HD)

    def new_weights(head):
        scores = scores_of(scaled_q[head], count)
        old = m_ref[head]
        top = jnp.maximum(old, jnp.max(scores, axis=1, keepdims=True))
        shrink = jnp.exp2(old - top)
        m_ref[head] = top
        return weigh(scores, top), jnp.concatenate([shrink, shrink], axis=1) * acc_ref[head]

    def attend_group(turn, source):
        def load(kv_head):
            load_keys(kv_head, group_rows(turn, 0, kv_head), keep_ref[source])
            load_values(group_rows(turn, 1, kv_head), keep_ref[source])

        def one_head(head):
            weights, kept = new_weights(head)
            acc_ref[head] = kept + jnp.dot(weights, value_block[...], preferred_element_type=jnp.float32)

        each_kv_head(load, one_head)

    def last_weights(turn, source):
        def load(kv_head):
            load_keys(kv_head, group_rows(turn, 0, kv_head), keep_ref[source])

        def one_head(head):
            weights, kept = new_weights(head)
            weights_ref[head] = weights
            acc_ref[head] = kept

        each_kv_head(load, one_head)

    def last_sums(turn, source):
        def load(kv_head):
            load_values(group_rows(turn, 1, kv_head), keep_ref[source])

        def one_head(head):
            summed = acc_ref[head] + jnp.dot(
                weights_ref[head], value_block[...], preferred_element_type=jnp.float32
            )
            o_ref[:, pl.ds(pl.multiple_of(head * HD, HD), HD)] = (summed[:, :HD] / summed[:, HD:]).astype(
                jnp.bfloat16
            )

        each_kv_head(load, one_head)

    pick_and_send(here, 0, 0, ck_ref)
    pick_and_send(here, 0, 1, cv_ref)
    attend_suffix()
    wait_plane(0, 0)
    wait_plane(0, 1)
    last = line - 1
    for turn in range(1, last):
        event(turn, 0)
        attend_group(turn - 1, here if turn == 1 else source_of(turn - 1, here, line))
        event(turn, 1)
        wait_plane(turn, 0)
        wait_plane(turn, 1)
    attend_group(last - 1, source_of(last - 1, here, line))
    last_source = source_of(last, here, line)
    event(last, 0)
    wait_plane(last, 0)
    last_weights(last, last_source)
    event(last, 1)
    wait_plane(last, 1)
    last_sums(last, last_source)

    for kind in range(2):
        for side in range(2):

            @pl.when(has_side[side])
            def _():
                own_copy(side, kind).wait_send()

            for far in range(1, line - 1):
                source = here - far if side == 0 else here + far
                valid = source >= 0 if side == 0 else source < line

                @pl.when(jnp.logical_and(valid, has_side[1 - side]))
                def _():
                    forward_copy(side, far, kind).wait_send()


def fused(queries, suf_keys, suf_values, cache_keys, cache_values, fetch_owner, fetch_page, prefix_len):
    host_count = lax.axis_size("hst")
    line = host_count // PLANE
    slot_count = fetch_owner.shape[1]
    capacity = slot_count // host_count
    own_pages, page_rows, kv_width = cache_keys.shape
    suffix = queries.shape[0]
    heads = queries.shape[1] // HD
    vmem = pl.BlockSpec(memory_space=pltpu.VMEM)
    chunk = capacity * page_rows
    shard = (own_pages, page_rows, kv_width)
    dma = pltpu.SemaphoreType.DMA
    return pl.pallas_call(
        functools.partial(fused_kernel, line, capacity, page_rows),
        out_shape=jax.ShapeDtypeStruct(queries.shape, jnp.bfloat16),
        in_specs=[vmem] * 7 + [pl.BlockSpec(memory_space=pltpu.SMEM)],
        out_specs=vmem,
        scratch_shapes=[
            pltpu.VMEM((8, slot_count), jnp.int32),
            pltpu.VMEM((PLANE, 8, slot_count), jnp.int32),
            pltpu.SMEM((PLANE, 8, slot_count), jnp.int32),
            pltpu.VMEM((line, PLANE * chunk, HD), jnp.bfloat16),
            pltpu.VMEM((2, line - 1, 2) + shard, jnp.bfloat16),
            pltpu.VMEM(shard, jnp.bfloat16),
            pltpu.VMEM((line, 2, PLANE - 1, chunk, kv_width), jnp.bfloat16),
            pltpu.VMEM((line, 2, PLANE, chunk, kv_width), jnp.bfloat16),
            pltpu.VMEM((heads, suffix, 2 * HD), jnp.bfloat16),
            pltpu.VMEM((2 * HD, PLANE * chunk) if TURN_KEYS else (PLANE * chunk, 2 * HD), jnp.bfloat16),
            pltpu.VMEM((PLANE * chunk, 2 * HD), jnp.bfloat16),
            pltpu.VMEM((heads, suffix, PLANE * chunk), jnp.bfloat16),
            pltpu.VMEM((heads, suffix, HD), jnp.float32),
            pltpu.VMEM((heads, suffix, 2 * HD), jnp.float32),
            dma((PLANE - 1,)),
            dma((PLANE,)),
            dma((2,)),
            dma((2, 2)),
            dma((2, line - 1, 2)),
            dma((2, line - 1, 2)),
            dma((line, 2, PLANE - 1)),
            dma((line, 2, PLANE)),
        ],
        compiler_params=pltpu.CompilerParams(
            collective_id=0, has_side_effects=True, vmem_limit_bytes=VMEM_BYTES
        ),
    )(queries, suf_keys, suf_values, cache_keys, cache_values, fetch_owner, fetch_page, prefix_len)


def fits(mesh, cache_shape):
    hosts = mesh.shape["hst"]
    own_bytes = 2 * 2 * cache_shape[1] * cache_shape[2] * cache_shape[0] // mesh.size
    return hosts % PLANE == 0 and hosts > PLANE and 2 * (hosts // PLANE - 1) * own_bytes <= 8 * 2**20


def solution(mesh):
    in_specs = (
        P(("dom", "hst"), None),
        P(("dom", "hst"), None),
        P(("dom", "hst"), None),
        P(("dom", "hst"), None, None),
        P(("dom", "hst"), None, None),
        P(("dom", "hst"), None),
        P(("dom", "hst"), None),
        P(("dom", "hst")),
    )
    out_specs = P(("dom", "hst"), None)

    def run(*args):
        body = fused if fits(mesh, args[3].shape) else shards
        return jax.shard_map(
            body, mesh=mesh, in_specs=in_specs, out_specs=out_specs, check_vma=False
        )(*args)

    return run
```

```python
import functools

import jax
import jax.numpy as jnp
from jax import lax
from jax.experimental import pallas as pl
from jax.experimental.pallas import tpu as pltpu
from jax.sharding import PartitionSpec as P

HD = 128


MASKED = -1e30


def partial_terms(query_rows, key_rows, value_rows, visible, score_scale):
    scores = (
        lax.dot_general(
            query_rows, key_rows, (((1,), (1,)), ((), ())), preferred_element_type=jnp.float32
        )
        * score_scale
    )
    scores = jnp.where(visible, scores, MASKED)
    row_max = jnp.max(scores, axis=1)
    weights = jnp.where(visible, jnp.exp(scores - row_max[:, None]), jnp.float32(0.0))
    weight_sum = jnp.sum(weights, axis=1)
    summed = jnp.dot(weights.astype(jnp.bfloat16), value_rows, preferred_element_type=jnp.float32)
    return (row_max, weight_sum, summed)


def blocked_terms(query_rows, row_token, key_rows, value_rows, visible_for, score_scale):
    row_count = query_rows.shape[0]
    block_rows = min(512, row_count)
    block_count = row_count // block_rows
    row_blocks = query_rows.reshape(block_count, block_rows, query_rows.shape[1])
    token_blocks = row_token.reshape(block_count, block_rows)

    def one_block(block_pair):
        return partial_terms(
            block_pair[0], key_rows, value_rows, visible_for(block_pair[1]), score_scale
        )

    row_max, weight_sum, summed = lax.map(one_block, (row_blocks, token_blocks))
    return (
        row_max.reshape(row_count),
        weight_sum.reshape(row_count),
        summed.reshape(row_count, -1),
    )


def shards(
    queries, suf_keys, suf_values, cache_keys, cache_values, fetch_owner, fetch_page, prefix_len
):
    host_count = lax.axis_size("hst")
    own_index = lax.axis_index("hst")
    slot_count = fetch_owner.shape[1]
    capacity = slot_count // host_count
    page_rows = cache_keys.shape[1]
    kv_width = cache_keys.shape[2]
    suffix = queries.shape[0]
    kv_heads = kv_width // HD
    group_size = queries.shape[1] // kv_width
    score_scale = HD ** (-0.5)
    owners = fetch_owner[0]
    length = prefix_len[0]
    peer_ids = jnp.arange(host_count, dtype=jnp.int32)
    owner_hits = (owners[:, None] == peer_ids[None, :]).astype(jnp.int32)
    before = jnp.cumsum(owner_hits, axis=0) - owner_hits
    owner_rank = jnp.sum(before * owner_hits, axis=1)
    slot_of = owners * capacity + owner_rank
    slot_ids = jnp.arange(slot_count, dtype=jnp.int32)
    slot_match = (slot_of[None, :] == slot_ids[:, None]).astype(jnp.int32)
    position = jnp.sum(slot_match * slot_ids[None, :], axis=1)
    all_owners, all_pages = (
        lax.all_gather(fetch_owner, "hst", axis=0, tiled=True),
        lax.all_gather(fetch_page, "hst", axis=0, tiled=True),
    )
    from_me = (all_owners == own_index).astype(jnp.int32)
    send_rank = jnp.cumsum(from_me, axis=1) - from_me
    level_ids = jnp.arange(capacity, dtype=jnp.int32)
    picked = from_me[:, :, None] * (send_rank[:, :, None] == level_ids[None, None, :]).astype(
        jnp.int32
    )
    served = jnp.sum(picked * all_pages[:, :, None], axis=1)
    flat_served = served.reshape(-1)
    sent_keys = cache_keys[flat_served].reshape(host_count, capacity, page_rows, kv_width)
    sent_values = cache_values[flat_served].reshape(host_count, capacity, page_rows, kv_width)
    row_token = jnp.arange(suffix * group_size, dtype=jnp.int32) // group_size
    suffix_ids = jnp.arange(suffix, dtype=jnp.int32)
    page_offsets = jnp.arange(page_rows, dtype=jnp.int32)
    head_rows = [
        queries[:, kv_head * group_size * HD : (kv_head + 1) * group_size * HD].reshape(
            suffix * group_size, HD
        )
        for kv_head in range(kv_heads)
    ]

    def causal_for(block_tokens):
        return suffix_ids[None, :] <= block_tokens[:, None]

    got_keys, got_values = (
        lax.all_to_all(
            sent_keys.reshape(host_count, capacity * page_rows, kv_width),
            "hst",
            split_axis=0,
            concat_axis=0,
            tiled=True,
        ),
        lax.all_to_all(
            sent_values.reshape(host_count, capacity * page_rows, kv_width),
            "hst",
            split_axis=0,
            concat_axis=0,
            tiled=True,
        ),
    )
    key_rows = jnp.concatenate(
        [got_keys.reshape(slot_count * page_rows, kv_width), suf_keys], axis=0
    )
    value_rows = jnp.concatenate(
        [got_values.reshape(slot_count * page_rows, kv_width), suf_values], axis=0
    )
    prefix_ok = (position[:, None] * page_rows + page_offsets[None, :]).reshape(-1) < length

    def visible_for(block_tokens):
        prefix_part = jnp.broadcast_to(
            prefix_ok[None, :], (block_tokens.shape[0], prefix_ok.shape[0])
        )
        return jnp.concatenate([prefix_part, causal_for(block_tokens)], axis=1)

    states = [
        blocked_terms(
            head_rows[kv_head],
            row_token,
            key_rows[:, kv_head * HD : (kv_head + 1) * HD],
            value_rows[:, kv_head * HD : (kv_head + 1) * HD],
            visible_for,
            score_scale,
        )
        for kv_head in range(kv_heads)
    ]
    results = [(state[2] / state[1][:, None]).reshape(suffix, group_size * HD) for state in states]
    return jnp.concatenate(results, axis=1).astype(jnp.bfloat16)


PLANE = 4
WIDTH = 8
TURN_KEYS = False
LOG2E = 1.4426950408889634
VMEM_BYTES = 56 * 2**20
MESH = pl.DeviceIdType.MESH


def arrival(source, here, line):
    far = jnp.abs(source - here)
    nearer = jnp.minimum(far - 1, here) + jnp.minimum(far - 1, line - 1 - here)
    after_twin = jnp.logical_and(source > here, here - far >= 0).astype(jnp.int32)
    return nearer + after_twin + 1


def source_of(turn, here, line):
    found = jnp.int32(0)
    for candidate in range(line):
        match = jnp.logical_and(candidate != here, arrival(jnp.int32(candidate), here, line) == turn)
        found = found + jnp.where(match, candidate, 0)
    return found


def fused_kernel(
    line,
    capacity,
    page_rows,
    q_ref,
    sk_ref,
    sv_ref,
    ck_ref,
    cv_ref,
    owner_ref,
    page_ref,
    len_ref,
    o_ref,
    table_ref,
    tables,
    pages_smem,
    keep_ref,
    line_buf,
    picked_from,
    stage,
    got,
    scaled_q,
    key_block,
    value_block,
    weights_ref,
    m_ref,
    acc_ref,
    table_send,
    table_recv,
    local_sem,
    own_send,
    line_send,
    line_recv,
    plane_send,
    plane_recv,
):
    me = lax.axis_index("hst")
    here = me // PLANE
    place = lax.rem(me, PLANE)
    suffix = q_ref.shape[0]
    heads = q_ref.shape[1] // HD
    kv_width = sk_ref.shape[1]
    group_heads = heads // (kv_width // HD)
    chunk = capacity * page_rows
    factor = HD ** (-0.5) * LOG2E
    caches = (ck_ref, cv_ref)

    def partner(step):
        return lax.rem(place + step, PLANE)

    def plane_id(where):
        return {"hst": here * PLANE + where}

    def line_id(where):
        return {"hst": where * PLANE + place}

    has_side = (here > 0, here < line - 1)
    toward = (here - 1, here + 1)

    barrier = pltpu.get_barrier_semaphore()
    for step in range(1, PLANE):
        pl.semaphore_signal(barrier, inc=1, device_id=plane_id(partner(step)), device_id_type=MESH)
    for side in range(2):

        @pl.when(has_side[side])
        def _():
            pl.semaphore_signal(barrier, inc=1, device_id=line_id(toward[side]), device_id_type=MESH)

    sides = has_side[0].astype(jnp.int32) + has_side[1].astype(jnp.int32)
    pl.semaphore_wait(barrier, PLANE - 1 + sides)

    def make_table():
        slots = owner_ref.shape[1]
        square = (slots, slots)
        down = lax.broadcasted_iota(jnp.int32, square, 0)
        across = lax.broadcasted_iota(jnp.int32, square, 1)
        owner_row = jnp.broadcast_to(owner_ref[...], square)
        owner_column = jnp.transpose(owner_row)
        page_column = jnp.transpose(jnp.broadcast_to(page_ref[...], square))
        same = owner_row == owner_column
        rank_row = jnp.sum(
            jnp.where(jnp.logical_and(same, down < across), 1, 0), axis=0, keepdims=True
        )
        slot_row = jnp.broadcast_to(owner_row[:1] * capacity + rank_row, square)
        slot_column = jnp.transpose(slot_row)
        pages = jnp.sum(
            jnp.where(slot_column == across, page_column, 0), axis=0, keepdims=True
        )
        pages = jnp.clip(pages, 0, ck_ref.shape[0] - 1)
        table_ref[...] = jnp.broadcast_to(pages, table_ref.shape)
        position = jnp.sum(
            jnp.where(slot_row == down, across, 0).astype(jnp.float32),
            axis=1,
            keepdims=True,
        )
        by_row = jnp.broadcast_to(position.reshape(slots, 1, 1), (slots, page_rows, HD))
        in_page = lax.broadcasted_iota(jnp.int32, by_row.shape, 1).astype(jnp.float32)
        limit = len_ref[0].astype(jnp.float32)
        keep = jnp.where(by_row * page_rows + in_page < limit, 1.0, 0.0).astype(jnp.bfloat16)
        keep_ref[...] = keep.reshape(keep_ref.shape)

    def own_copy(side, kind):
        return pltpu.make_async_remote_copy(
            src_ref=caches[kind],
            dst_ref=line_buf.at[1 - side, 0, kind],
            send_sem=own_send.at[side, kind],
            recv_sem=line_recv.at[1 - side, 0, kind],
            device_id=line_id(toward[side]),
            device_id_type=MESH,
        )

    def forward_copy(side, far, kind):
        return pltpu.make_async_remote_copy(
            src_ref=line_buf.at[side, far - 1, kind],
            dst_ref=line_buf.at[side, far, kind],
            send_sem=line_send.at[side, far - 1, kind],
            recv_sem=line_recv.at[side, far, kind],
            device_id=line_id(toward[1 - side]),
            device_id_type=MESH,
        )

    def table_copy(step):
        return pltpu.make_async_remote_copy(
            src_ref=table_ref,
            dst_ref=tables.at[place],
            send_sem=table_send.at[step - 1],
            recv_sem=table_recv.at[place],
            device_id=plane_id(partner(step)),
            device_id_type=MESH,
        )

    def plane_copy(turn, kind, step):
        return pltpu.make_async_remote_copy(
            src_ref=stage.at[turn, kind, step - 1],
            dst_ref=got.at[turn, kind, place],
            send_sem=plane_send.at[turn, kind, step - 1],
            recv_sem=plane_recv.at[turn, kind, place],
            device_id=plane_id(partner(step)),
            device_id_type=MESH,
        )

    for kind in range(2):
        for side in range(2):

            @pl.when(has_side[side])
            def _():
                own_copy(side, kind).start()

    make_table()
    for step in range(1, PLANE):
        table_copy(step).start()

    own_table = pltpu.make_async_copy(table_ref, tables.at[place], local_sem.at[0])
    own_table.start()
    own_table.wait()
    for step in range(1, PLANE):
        from_there = pltpu.make_async_remote_copy(
            src_ref=table_ref,
            dst_ref=tables.at[partner(step)],
            send_sem=table_send.at[step - 1],
            recv_sem=table_recv.at[partner(step)],
            device_id=plane_id(partner(step)),
            device_id_type=MESH,
        )
        from_there.wait()
    to_smem = pltpu.make_async_copy(tables, pages_smem, local_sem.at[1])
    to_smem.start()
    to_smem.wait()

    def pick_and_send(source, turn, kind, from_ref):
        first = (source * PLANE + place) * capacity
        for step in range(1, PLANE):
            who = partner(step)

            def one_page(j, carry):
                page = pages_smem[who, 0, first + j]
                stage[turn, kind, step - 1, pl.ds(pl.multiple_of(j * page_rows, page_rows), page_rows)] = (
                    from_ref[page]
                )
                return carry

            lax.fori_loop(0, capacity, one_page, 0, unroll=True)
            plane_copy(turn, kind, step).start()

        def own_page(j, carry):
            page = pages_smem[place, 0, first + j]
            got[turn, kind, place, pl.ds(pl.multiple_of(j * page_rows, page_rows), page_rows)] = from_ref[
                page
            ]
            return carry

        lax.fori_loop(0, capacity, own_page, 0, unroll=True)

    def event(far, kind):
        for side in range(2):
            source = here - far if side == 0 else here + far
            valid = source >= 0 if side == 0 else source < line

            @pl.when(valid)
            def _():
                pltpu.make_async_remote_copy(
                    src_ref=line_buf.at[side, far - 1, kind],
                    dst_ref=line_buf.at[side, far - 1, kind],
                    send_sem=line_send.at[side, far - 1, kind],
                    recv_sem=line_recv.at[side, far - 1, kind],
                    device_id=line_id(source),
                    device_id_type=MESH,
                ).wait_recv()
                if far < line - 1:

                    @pl.when(has_side[1 - side])
                    def _():
                        forward_copy(side, far, kind).start()

                picked_from[...] = line_buf[side, far - 1, kind]
                pick_and_send(source, arrival(source, here, line), kind, picked_from)

    def wait_plane(turn, kind):
        for step in range(1, PLANE):
            there = partner(step)
            pltpu.make_async_remote_copy(
                src_ref=stage.at[turn, kind, step - 1],
                dst_ref=got.at[turn, kind, there],
                send_sem=plane_send.at[turn, kind, step - 1],
                recv_sem=plane_recv.at[turn, kind, there],
                device_id=plane_id(there),
                device_id_type=MESH,
            ).wait()

    kv_heads = kv_width // HD
    count = PLANE * chunk

    def load_keys(kv_head, key_rows, keep):
        if keep is not None:
            columns = pl.ds(pl.multiple_of(kv_head * HD, HD), HD)
            key_rows = key_rows * keep + sk_ref[0:1, columns] * (1 - keep)
        if TURN_KEYS:
            turned = jnp.transpose(key_rows)
            key_block[0:HD, : key_rows.shape[0]] = turned
            key_block[HD : 2 * HD, : key_rows.shape[0]] = turned
        else:
            key_block[: key_rows.shape[0], :HD] = key_rows
            key_block[: key_rows.shape[0], HD:] = key_rows

    def load_values(value_rows, keep):
        rows = value_rows.shape[0]
        value_block[:rows, :HD] = value_rows if keep is None else value_rows * keep
        value_block[:rows, HD:] = jnp.ones_like(value_rows) if keep is None else keep

    def scores_of(query_rows, keys):
        if TURN_KEYS:
            return jnp.dot(query_rows, key_block[:, :keys], preferred_element_type=jnp.float32)
        return lax.dot_general(
            query_rows, key_block[:keys], (((1,), (1,)), ((), ())), preferred_element_type=jnp.float32
        )

    def each_kv_head(load, one_head, part=(0, kv_heads)):
        def kv_step(kv_head, carry):
            load(kv_head)

            def heads_step(part, inner_carry):
                for inner in range(WIDTH):
                    one_head(kv_head * group_heads + part * WIDTH + inner)
                return inner_carry

            lax.fori_loop(0, group_heads // WIDTH, heads_step, 0)
            return carry

        lax.fori_loop(part[0], part[1], kv_step, 0)

    def weigh(scores, top):
        return jnp.concatenate(
            [
                jnp.exp2(scores[:, tile * HD : (tile + 1) * HD] - top).astype(jnp.bfloat16)
                for tile in range(scores.shape[1] // HD)
            ],
            axis=1,
        )

    def attend_suffix():
        causal = lax.broadcasted_iota(jnp.int32, (suffix, suffix), 1) <= lax.broadcasted_iota(
            jnp.int32, (suffix, suffix), 0
        )

        def load(kv_head):
            columns = pl.ds(pl.multiple_of(kv_head * HD, HD), HD)
            load_keys(kv_head, sk_ref[:, columns], None)
            load_values(sv_ref[:, columns], None)

        def one_head(head):
            scaled = q_ref[:, pl.ds(pl.multiple_of(head * HD, HD), HD)].astype(jnp.float32) * factor
            high = scaled.astype(jnp.bfloat16)
            low = (scaled - high.astype(jnp.float32)).astype(jnp.bfloat16)
            both = jnp.concatenate([high, low], axis=1)
            scaled_q[head] = both
            scores = jnp.where(causal, scores_of(both, suffix), MASKED)
            top = jnp.broadcast_to(jnp.max(scores, axis=1, keepdims=True), (suffix, HD))
            weights = weigh(scores, top)
            m_ref[head] = top
            acc_ref[head] = jnp.dot(weights, value_block[:suffix], preferred_element_type=jnp.float32)

        each_kv_head(load, one_head)

    def group_rows(turn, kind, kv_head):
        columns = pl.ds(pl.multiple_of(kv_head * HD, HD), HD)
        return got[turn, kind, :, :, columns].reshape(count, HD)

    def new_weights(head):
        scores = scores_of(scaled_q[head], count)
        old = m_ref[head]
        top = jnp.maximum(old, jnp.max(scores, axis=1, keepdims=True))
        shrink = jnp.exp2(old - top)
        m_ref[head] = top
        return weigh(scores, top), jnp.concatenate([shrink, shrink], axis=1) * acc_ref[head]

    def attend_group(turn, source, part=(0, kv_heads)):
        def load(kv_head):
            load_keys(kv_head, group_rows(turn, 0, kv_head), keep_ref[source])
            load_values(group_rows(turn, 1, kv_head), keep_ref[source])

        def one_head(head):
            weights, kept = new_weights(head)
            acc_ref[head] = kept + jnp.dot(weights, value_block[...], preferred_element_type=jnp.float32)

        each_kv_head(load, one_head, part)

    def last_weights(turn, source, part):
        def load(kv_head):
            load_keys(kv_head, group_rows(turn, 0, kv_head), keep_ref[source])

        def one_head(head):
            weights, kept = new_weights(head)
            weights_ref[head] = weights
            acc_ref[head] = kept

        each_kv_head(load, one_head, part)

    def last_sums(turn, source):
        def load(kv_head):
            load_values(group_rows(turn, 1, kv_head), keep_ref[source])

        def one_head(head):
            summed = acc_ref[head] + jnp.dot(
                weights_ref[head], value_block[...], preferred_element_type=jnp.float32
            )
            o_ref[:, pl.ds(pl.multiple_of(head * HD, HD), HD)] = (summed[:, :HD] / summed[:, HD:]).astype(
                jnp.bfloat16
            )

        each_kv_head(load, one_head)

    pick_and_send(here, 0, 0, ck_ref)
    pick_and_send(here, 0, 1, cv_ref)
    attend_suffix()
    wait_plane(0, 0)
    wait_plane(0, 1)
    last = line - 1
    for turn in range(1, last):
        event(turn, 0)
        attend_group(turn - 1, here if turn == 1 else source_of(turn - 1, here, line))
        event(turn, 1)
        wait_plane(turn, 0)
        wait_plane(turn, 1)
    halves = ((0, kv_heads // 2), (kv_heads // 2, kv_heads))
    last_source = source_of(last, here, line)
    before = source_of(last - 1, here, line)
    attend_group(last - 1, before, halves[0])
    event(last, 0)
    attend_group(last - 1, before, halves[1])
    wait_plane(last, 0)
    last_weights(last, last_source, halves[0])
    event(last, 1)
    last_weights(last, last_source, halves[1])
    wait_plane(last, 1)
    last_sums(last, last_source)

    for kind in range(2):
        for side in range(2):

            @pl.when(has_side[side])
            def _():
                own_copy(side, kind).wait_send()

            for far in range(1, line - 1):
                source = here - far if side == 0 else here + far
                valid = source >= 0 if side == 0 else source < line

                @pl.when(jnp.logical_and(valid, has_side[1 - side]))
                def _():
                    forward_copy(side, far, kind).wait_send()


def fused(queries, suf_keys, suf_values, cache_keys, cache_values, fetch_owner, fetch_page, prefix_len):
    host_count = lax.axis_size("hst")
    line = host_count // PLANE
    slot_count = fetch_owner.shape[1]
    capacity = slot_count // host_count
    own_pages, page_rows, kv_width = cache_keys.shape
    suffix = queries.shape[0]
    heads = queries.shape[1] // HD
    vmem = pl.BlockSpec(memory_space=pltpu.VMEM)
    chunk = capacity * page_rows
    shard = (own_pages, page_rows, kv_width)
    dma = pltpu.SemaphoreType.DMA
    return pl.pallas_call(
        functools.partial(fused_kernel, line, capacity, page_rows),
        out_shape=jax.ShapeDtypeStruct(queries.shape, jnp.bfloat16),
        in_specs=[vmem] * 7 + [pl.BlockSpec(memory_space=pltpu.SMEM)],
        out_specs=vmem,
        scratch_shapes=[
            pltpu.VMEM((8, slot_count), jnp.int32),
            pltpu.VMEM((PLANE, 8, slot_count), jnp.int32),
            pltpu.SMEM((PLANE, 8, slot_count), jnp.int32),
            pltpu.VMEM((line, PLANE * chunk, HD), jnp.bfloat16),
            pltpu.VMEM((2, line - 1, 2) + shard, jnp.bfloat16),
            pltpu.VMEM(shard, jnp.bfloat16),
            pltpu.VMEM((line, 2, PLANE - 1, chunk, kv_width), jnp.bfloat16),
            pltpu.VMEM((line, 2, PLANE, chunk, kv_width), jnp.bfloat16),
            pltpu.VMEM((heads, suffix, 2 * HD), jnp.bfloat16),
            pltpu.VMEM((2 * HD, PLANE * chunk) if TURN_KEYS else (PLANE * chunk, 2 * HD), jnp.bfloat16),
            pltpu.VMEM((PLANE * chunk, 2 * HD), jnp.bfloat16),
            pltpu.VMEM((heads, suffix, PLANE * chunk), jnp.bfloat16),
            pltpu.VMEM((heads, suffix, HD), jnp.float32),
            pltpu.VMEM((heads, suffix, 2 * HD), jnp.float32),
            dma((PLANE - 1,)),
            dma((PLANE,)),
            dma((2,)),
            dma((2, 2)),
            dma((2, line - 1, 2)),
            dma((2, line - 1, 2)),
            dma((line, 2, PLANE - 1)),
            dma((line, 2, PLANE)),
        ],
        compiler_params=pltpu.CompilerParams(
            collective_id=0, has_side_effects=True, vmem_limit_bytes=VMEM_BYTES
        ),
    )(queries, suf_keys, suf_values, cache_keys, cache_values, fetch_owner, fetch_page, prefix_len)


def fits(mesh, cache_shape):
    hosts = mesh.shape["hst"]
    own_bytes = 2 * 2 * cache_shape[1] * cache_shape[2] * cache_shape[0] // mesh.size
    return hosts % PLANE == 0 and hosts > PLANE and 2 * (hosts // PLANE - 1) * own_bytes <= 8 * 2**20


def solution(mesh):
    in_specs = (
        P(("dom", "hst"), None),
        P(("dom", "hst"), None),
        P(("dom", "hst"), None),
        P(("dom", "hst"), None, None),
        P(("dom", "hst"), None, None),
        P(("dom", "hst"), None),
        P(("dom", "hst"), None),
        P(("dom", "hst")),
    )
    out_specs = P(("dom", "hst"), None)

    def run(*args):
        body = fused if fits(mesh, args[3].shape) else shards
        return jax.shard_map(
            body, mesh=mesh, in_specs=in_specs, out_specs=out_specs, check_vma=False
        )(*args)

    return run
```
